256 devices in a mesh: dp: 32 (over z, y_lo, core), mp: 8 (over x, y_hi).
Axes of the slice: x: 4, y: 4 (y_hi: 2, y_lo: 2; y = y_hi * 2 + y_lo), z: 8, core: 2. Of those that a mesh axis runs over, the one named last changes fastest.
Arguments:
- attn_heads: bfloat16 [12288, 8192], P('dp', 'mp'), may hold values from -6 to 6
- out_proj: bfloat16 [8192, 8192], P('mp', 'dp'), may hold values from -0.0625 to 0.0625
- teacher_resid: bfloat16 [12288, 8192], P('dp', 'mp'), may hold values from -6 to 6
- student_in: bfloat16 [12288, 3072], P('dp'), may hold values from -6 to 6
- norm_gain: bfloat16 [3072], replicated, may hold values from 0.099609375 to 1.8984375
- projector: bfloat16 [3072, 8192], P(None, 'mp'), may hold values from -0.109375 to 0.109375
Outputs:
- grad_proj: float32 [3072, 8192], P('dp', 'mp')
- student_hidden_gradient: bfloat16 [12288, 3072], P('dp', 'mp')
The draws below stay inside these ranges and needn't reach their ends.
All inputs are finite; a program needn't handle non-finite values.
Results may differ from the reference program's by a relative error of at most 0.029.
Values may be sent and summed in bfloat16 or wider, within the bound.
No kernel may reach another device: no remote copies, remote signals or barrier semaphores. Data moves between devices by JAX's collectives and lax.ppermute only.
A program may use at most 128 MiB of HBM per device.

```python
import math
import jax
import jax.numpy as jnp
from jax import lax

D = 8192
SD = 3072
TOK_DEV = 384
TOKENS = 12288
N_DP = 32
N_MP = 8


def strengthened(result, key, source, target, parts, factor):
    def block_of(position):
        return (jnp.arange(result.shape[position]) // (result.shape[position] // parts)).reshape((-1,) + (1,) * (result.ndim - 1 - position))

    near = jax.random.permutation(key, parts)[block_of(target)]
    other_side = (block_of(target) + parts // 2) % parts
    return jnp.where((block_of(source) == near) | (block_of(source) == other_side), factor * result, result)


def block_levels(key, shape, split, low, top_value):
    def one(dim, blocks):
        steps = jax.random.uniform(jax.random.fold_in(jax.random.fold_in(key, 6), dim), (blocks,), jnp.float32, low / len(split), top_value / len(split))
        return jnp.repeat(jnp.exp(steps), shape[dim] // blocks).reshape((-1,) + (1,) * (len(shape) - dim - 1))

    gain = one(*split[0])
    for cut in split[1:]:
        gain = gain * one(*cut)
    return gain


def normal_values(key, extent, deviation, most, cuts=(), held_as=jnp.bfloat16):
    entries = jax.random.normal(key, extent, jnp.float32) * deviation
    if len(cuts) > 0:
        entries = block_levels(key, extent, cuts, -0.22, 0.18) * entries
    return jnp.clip(entries, min=-most, max=most).astype(held_as)


def noise_with(stream_key, shape, deviation, most, split, heavy, kind=jnp.bfloat16):
    result = deviation * jax.random.normal(stream_key, shape, jnp.float32)
    if split:
        result = result * block_levels(stream_key, shape, split, -0.22, 0.18)
    return jnp.clip(strengthened(result, jax.random.fold_in(stream_key, 3), *heavy), -most, most).astype(kind)


def setup_inputs(seed: int = 0) -> dict:
    streams_of = jax.random.split(jax.random.key(seed), 7)
    attn_heads = normal_values(streams_of[0], (TOKENS, D), 1.0, 6.0, ((0, 32), (1, 8)))
    out_proj = normal_values(streams_of[1], (D, D), D ** -0.5, 0.0625, ((0, 8), (1, 32)))
    teacher_resid = normal_values(streams_of[2], (TOKENS, D), 1.0, 6.0, ((0, 32), (1, 8)))
    student_in = noise_with(streams_of[3], (TOKENS, SD), 1.0, 6.0, ((0, 32),), (0, 1, 32, 2.75))
    norm_gain = jnp.clip(1.0 + 0.18 * jax.random.normal(streams_of[4], (SD,), jnp.float32), 0.099609375, 1.8984375).astype(jnp.bfloat16)
    projector = normal_values(streams_of[5], (SD, D), SD ** -0.5, 0.109375, ((1, 8),))
    return {"attn_heads": attn_heads, "out_proj": out_proj, "teacher_resid": teacher_resid, "student_in": student_in, "norm_gain": norm_gain, "projector": projector}


def reference(attn_heads, out_proj, teacher_resid, student_in, norm_gain, projector):
    width = D // N_MP
    sums = jnp.zeros((TOKENS, D), jnp.float32)
    for group in range(N_MP):
        part = jnp.dot(attn_heads[:, group * width:(group + 1) * width], out_proj[group * width:(group + 1) * width, :], preferred_element_type=jnp.float32)
        part = lax.optimization_barrier(part.astype(jnp.bfloat16))
        sums = sums + part.astype(jnp.float32)
    target = (sums + teacher_resid.astype(jnp.float32)).astype(jnp.bfloat16)
    value_entries = student_in.astype(jnp.float32)
    inverse_root = lax.rsqrt(lax.optimization_barrier(jnp.mean(value_entries * value_entries, axis=-1, keepdims=True)) + 1e-05)
    normalized_input = value_entries * inverse_root
    norm_scale_vector = norm_gain.astype(jnp.float32)
    normalized_hidden = (normalized_input * norm_scale_vector).astype(jnp.bfloat16)
    z_full = jnp.dot(normalized_hidden, projector, preferred_element_type=jnp.float32)
    diff = (z_full - target.astype(jnp.float32)).astype(jnp.bfloat16)
    scale = 1.0 / math.sqrt(TOKENS)
    grad_proj = jnp.zeros((SD, D), jnp.float32)
    for slab in range(N_DP):
        rows_a = normalized_hidden[slab * TOK_DEV:(slab + 1) * TOK_DEV]
        rows_b = diff[slab * TOK_DEV:(slab + 1) * TOK_DEV]
        term = lax.dot_general(rows_a, rows_b, (((0,), (0,)), ((), ())), preferred_element_type=jnp.float32) * scale
        term = lax.optimization_barrier(term.astype(jnp.bfloat16))
        grad_proj = grad_proj + term.astype(jnp.float32)
    grad_normed = jnp.zeros((TOKENS, SD), jnp.float32)
    for group in range(N_MP):
        back = lax.dot_general(diff[:, group * width:(group + 1) * width], projector[:, group * width:(group + 1) * width], (((1,), (1,)), ((), ())), preferred_element_type=jnp.float32)
        back = lax.optimization_barrier(back.astype(jnp.bfloat16))
        grad_normed = grad_normed + back.astype(jnp.float32)
    normalized_gradient = grad_normed * norm_scale_vector
    squared_mean = lax.optimization_barrier(jnp.mean(normalized_gradient * normalized_input, axis=-1, keepdims=True))
    student_hidden_gradient = (inverse_root * (normalized_gradient - normalized_input * squared_mean)).astype(jnp.bfloat16)
    return (grad_proj, student_hidden_gradient)
```

```python
import math

import jax
import jax.numpy as jnp
from jax import lax
from jax.sharding import PartitionSpec as P

NZ, NX = 8, 4
BF, F32 = jnp.bfloat16, jnp.float32


def flat(z, l, c, x, h):
    return ((z * 2 + l) * 2 + c) * (NX * 2) + x * 2 + h


PLACES = [
    (z, l, c, x, h)
    for z in range(NZ)
    for l in range(2)
    for c in range(2)
    for x in range(NX)
    for h in range(2)
]


def move(value, to):
    return lax.ppermute(value, ("dp", "mp"), [(flat(*p), flat(*to(*p))) for p in PLACES])


def flip(value, a=0, b=0, e=0):
    return move(value, lambda z, l, c, x, h: (z, l ^ a, c ^ e, x, h ^ b))


def shift(value, s=0, k=0, b=0):
    return move(value, lambda z, l, c, x, h: ((z + s) % NZ, l, c, (x + k) % NX, h ^ b))


def after(value, *first):
    return lax.optimization_barrier((value, *first))[0]


def dot(a, b, dims):
    return lax.dot_general(a, b, (dims, ((), ())), preferred_element_type=F32)


def piece(value, index, size, axis):
    return lax.dynamic_slice_in_dim(value, index * size, size, axis)


def put(whole, value, index, axis):
    return lax.dynamic_update_slice_in_dim(whole, value, index * value.shape[axis], axis)


def on_device(attn, out_proj, resid, student, gain, projector):
    toks, wide = resid.shape
    sd = student.shape[1]
    blk = out_proj.shape[1]
    dp, mp = lax.axis_index("dp"), lax.axis_index("mp")
    z, l, c = dp // 4, (dp // 2) % 2, dp % 2
    x, h = mp // 2, mp % 2
    own_half = c == h

    w0 = move(
        out_proj,
        lambda z, l, c, x, h: (z, l, c, x, h) if c == h else (z, l, h, x, 1 - h),
    )

    v = student.astype(F32)
    inv = lax.rsqrt(jnp.mean(v * v, axis=-1, keepdims=True) + 1e-05)
    gain_f = gain.astype(F32)
    normed = (v * inv * gain_f).astype(BF)
    z_own = dot(normed, projector, ((1,), (0,)))
    d0 = (z_own - resid.astype(F32)).astype(BF)

    attn = after(attn, w0)
    a_h = flip(attn, b=1)
    a_l = flip(attn, a=1)
    a_lh = flip(attn, a=1, b=1)
    first = jnp.concatenate([jnp.where(own_half, attn, a_h), jnp.where(own_half, a_l, a_lh)], 0)
    second = jnp.concatenate([jnp.where(own_half, a_h, attn), jnp.where(own_half, a_lh, a_l)], 0)
    heads = jnp.concatenate([first, second], 1)

    d0_t = {}
    for a in range(2):
        for b in range(2):
            p = piece(d0, 2 * (l ^ a) + (h ^ b), blk, 1)
            d0_t[a, b] = flip(after(p, a_h), a=a, b=b) if a + b else p

    part = flip(after(piece(normed, x, toks // NX, 0), a_h), a=1)
    other = put(jnp.zeros((toks, sd), BF), part, x, 0)
    for k in range(1, NX):
        other = put(other, shift(part, k=k), (x - k) % NX, 0)
    both = jnp.concatenate([normed, other], 0)
    normed_all = jnp.concatenate([both, flip(both, e=1)], 0)

    got = {0: w0}
    half = w0.shape[0] // 2
    for s in range(1, 4):
        got[s] = shift(got[s - 1], s=-1)
        got[-s] = shift(got[-s + 1], s=1)
    got[4] = jnp.concatenate([shift(got[3][:half], s=-1), shift(got[-3][half:], s=1)], 0)
    outs = jnp.zeros((NZ, 2 * toks, blk), BF)
    for s in (0, 1, -1, 2, -2, 3, -3, 4):
        w = jnp.concatenate([got[s], flip(got[s], e=1)], 0)
        o = dot(heads, w, ((1,), (0,))).astype(BF)
        outs = put(outs, o[None], (z + s) % NZ, 0)

    total = piece(outs, x, 2, 0).astype(F32)
    for k in range(1, NX):
        total = total + shift(piece(outs, (x + k) % NX, 2, 0), k=k).astype(F32)
    diff_t = {}
    for b in range(2):
        t = lax.dynamic_index_in_dim(total, h ^ b, 0, keepdims=False)
        for a in range(2):
            diff_t[a, b] = (d0_t[a, b].astype(F32) - t[a * toks:(a + 1) * toks]).astype(BF)

    diff = jnp.zeros((toks, wide), BF)
    for a in range(2):
        for b in range(2):
            p = flip(diff_t[a, b], a=a, b=b) if a + b else diff_t[a, b]
            diff = put(diff, p, 2 * (l ^ a) + (h ^ b), 1)
    stat = lax.psum(jnp.sum(diff.astype(F32) * z_own, axis=-1), "mp") / sd

    stay = jnp.concatenate([diff_t[0, 0], diff_t[1, 0]], 0)
    leave = jnp.concatenate([diff_t[0, 1], diff_t[1, 1]], 0)
    stay, leave = jnp.where(own_half, stay, leave), jnp.where(own_half, leave, stay)
    cols = jnp.concatenate([stay, flip(leave, e=1)], 0)
    scale = 1.0 / math.sqrt(toks * NZ * 4)
    term = (dot(normed_all, cols, ((0,), (0,))) * scale).astype(BF)
    rows = sd // NZ
    grad = piece(term, z, rows, 0).astype(F32)
    for s in range(1, NZ):
        grad = grad + shift(piece(term, (z + s) % NZ, rows, 0), s=s).astype(F32)
    grad_proj = jnp.zeros((rows // 4, wide), F32)
    for a in range(2):
        for e in range(2):
            p = piece(grad, 2 * (l ^ a) + (h ^ e), rows // 4, 0)
            p = move(p, lambda z, l, c, x, h: (z, l ^ a, h ^ e, x, c))
            grad_proj = put(grad_proj, p, 2 * (l ^ a) + (c ^ e), 1)

    share = sd // (NX * 2)
    back = jnp.zeros((toks, share), F32)
    for k in range(NX):
        for b in range(2):
            f = 2 * ((x + k) % NX) + (h ^ b)
            p = dot(diff, piece(projector, f, share, 0), ((1,), (1,))).astype(BF)
            back = back + (shift(p, k=k, b=b) if k + b else p).astype(F32)
    xhat = piece(student, mp, share, 1).astype(F32) * inv
    dxhat = back * piece(gain_f, mp, share, 0)
    return grad_proj, (inv * (dxhat - xhat * stat[:, None])).astype(BF)


def solution(mesh):
    in_specs = (P("dp", "mp"), P("mp", "dp"), P("dp", "mp"), P("dp", None), P(), P(None, "mp"))
    out_specs = (P("dp", "mp"), P("dp", "mp"))
    return jax.shard_map(
        on_device, mesh=mesh, in_specs=in_specs, out_specs=out_specs, check_vma=False
    )
```

```python
import functools
import math

import jax
import jax.numpy as jnp
from jax import lax
from jax.experimental import pallas as pl
from jax.experimental.pallas import tpu as pltpu
from jax.sharding import PartitionSpec as P

NZ, NX = 8, 4
VMEM = 56 * 2**20
BF, F32 = jnp.bfloat16, jnp.float32


def flat(z, l, c, x, h):
    return ((z * 2 + l) * 2 + c) * (NX * 2) + x * 2 + h


PLACES = [
    (z, l, c, x, h)
    for z in range(NZ)
    for l in range(2)
    for c in range(2)
    for x in range(NX)
    for h in range(2)
]


RINGS = [[z * 4 + i for z in range(NZ)] for i in range(4)]
LINES = [[x * 2 + h for x in range(NX)] for h in range(2)]
SQUARES = [
    [flat(z, l, c, x, h) for l in range(2) for h in range(2)]
    for z in range(NZ)
    for c in range(2)
    for x in range(NX)
]


def move(value, to):
    return lax.ppermute(value, ("dp", "mp"), [(flat(*p), flat(*to(*p))) for p in PLACES])


def flip(value, a=0, b=0, e=0):
    if not a + b + e:
        return value
    return move(value, lambda z, l, c, x, h: (z, l ^ a, c ^ e, x, h ^ b))


def shift(value, s=0, k=0, b=0):
    return move(value, lambda z, l, c, x, h: ((z + s) % NZ, l, c, (x + k) % NX, h ^ b))


def after(value, *first):
    return lax.optimization_barrier((value, *first))[0]


def gate(*values):
    return lax.optimization_barrier(values)


def dot(a, b, dims):
    return lax.dot_general(a, b, (dims, ((), ())), preferred_element_type=F32)


def piece(value, index, size, axis):
    return lax.dynamic_slice_in_dim(value, index * size, size, axis)


def put(whole, value, index, axis):
    return lax.dynamic_update_slice_in_dim(whole, value, index * value.shape[axis], axis)


def difference_kernel(at, m0, m1, m2, m3, d0, stay, leave, *pieces):
    l, h, c = at[0], at[1], at[2]
    for b in range(2):
        for a in range(2):
            own = 2 * b + a
            total = m0[own].astype(F32) + m1[own].astype(F32) + m2[own].astype(F32) + m3[own].astype(F32)
            diff = (d0[2 * (l ^ a) + (h ^ b)].astype(F32) - total).astype(BF)
            pieces[2 * b + a][...] = diff

            @pl.when((h ^ b) == c)
            def _():
                stay[a] = diff

            @pl.when((h ^ b) != c)
            def _():
                leave[a] = diff


def difference(at, sums, d0):
    one = jax.ShapeDtypeStruct(d0.shape[1:], BF)
    two = jax.ShapeDtypeStruct((2, *d0.shape[1:]), BF)
    return pl.pallas_call(
        difference_kernel,
        out_shape=[two, two, one, one, one, one],
        grid=(1,),
        in_specs=[pl.BlockSpec(memory_space=pltpu.SMEM)] + [whole(d0.shape)] * 5,
        out_specs=[whole(two.shape)] * 2 + [whole(one.shape)] * 4,
        compiler_params=pltpu.CompilerParams(vmem_limit_bytes=VMEM),
    )(at, *sums, d0)


def whole(shape):
    return pl.BlockSpec(shape, lambda *i: (0,) * len(shape))


def products_kernel(n, kept, at, *refs):
    attn, a_h, a_l, a_lh = refs[kept:kept + 4]
    blocks = refs[kept + 4:kept + 4 + 2 * n]
    outs, (made, sems) = refs[kept + 4 + 2 * n:-2], refs[-2:]
    toks = attn.shape[0]

    def run(turn):
        for i in range(n):
            w_h, w_o = blocks[2 * i + turn], blocks[2 * i + 1 - turn]
            for a, (near, far) in enumerate(((attn, a_h), (a_l, a_lh))):
                part = jnp.dot(near[...], w_h[...], preferred_element_type=F32)
                part = part + jnp.dot(far[...], w_o[...], preferred_element_type=F32)
                made[i, a * toks:(a + 1) * toks] = part.astype(BF)

    pl.when(at[0] == 0)(lambda: run(0))
    pl.when(at[0] != 0)(lambda: run(1))
    for i in range(n):
        for k in range(NX):

            @pl.when(at[1 + 2 * i] == k)
            def _():
                copy = pltpu.make_async_copy(made.at[i], outs[k].at[at[2 + 2 * i]], sems.at[i])
                copy.start()
                copy.wait()


def products(at, kept, heads, blocks):
    n = len(blocks) // 2
    toks, blk = heads[0].shape[0], blocks[0].shape[1]
    anywhere = pl.BlockSpec(memory_space=pl.ANY)
    return pl.pallas_call(
        functools.partial(products_kernel, n, len(kept)),
        out_shape=[jax.ShapeDtypeStruct((2, 2 * toks, blk), BF)] * NX,
        grid=(1,),
        in_specs=[pl.BlockSpec(memory_space=pltpu.SMEM)]
        + [anywhere] * len(kept)
        + [whole(m.shape) for m in (*heads, *blocks)],
        out_specs=[anywhere] * NX,
        scratch_shapes=[pltpu.VMEM((n, 2 * toks, blk), BF), pltpu.SemaphoreType.DMA((n,))],
        input_output_aliases={1 + k: k for k in range(len(kept))},
        compiler_params=pltpu.CompilerParams(vmem_limit_bytes=VMEM),
        cost_estimate=pl.CostEstimate(
            flops=n * 8 * toks * blk * heads[0].shape[1], bytes_accessed=8 * 2**20, transcendentals=0
        ),
    )(at, *kept, *heads, *blocks)


def back_kernel(sd, at, d0, d1, d2, d3, z_own, rows_p, *refs):
    outs, (tail, turned) = refs[:-2], refs[-2:]
    share = rows_p.shape[0]
    step = pl.program_id(0)
    toks, blk = d0.shape
    columns = [pl.ds(pl.multiple_of(at[8 + q] * blk, blk), blk) for q in range(4)]
    pieces = (d0, d1, d2, d3)

    @pl.when(step == 0)
    def _():
        stat = 0.0
        for d, q in zip(pieces, columns):
            turned[q] = d[...].astype(F32).T.astype(BF)
            stat = stat + jnp.sum(d[...].astype(F32) * z_own[:, q], axis=-1, keepdims=True)
        stat = jnp.broadcast_to(stat / sd, (toks, 128)).T[:16]
        high = stat.astype(BF)
        low = (stat - high.astype(F32)).astype(BF)
        row = lax.broadcasted_iota(jnp.int32, stat.shape, 0)
        kept = jnp.where(row == 0, high.astype(F32), jnp.where(row == 1, low.astype(F32), 0.0))
        tail[...] = kept.astype(BF)

    part = jnp.dot(rows_p[...], turned[...], preferred_element_type=F32)
    for k, out in enumerate(outs):

        @pl.when(step == k)
        def _():
            out[:share] = part.astype(BF)
            out[share:] = tail[...]


def backs(at, diffs, z_own, projector, share):
    toks, blk = diffs[0].shape
    sd, wide = projector.shape
    one = jax.ShapeDtypeStruct((share + 16, toks), BF)
    return pl.pallas_call(
        functools.partial(back_kernel, sd),
        out_shape=[one] * 8,
        grid_spec=pltpu.PrefetchScalarGridSpec(
            num_scalar_prefetch=1,
            grid=(8,),
            in_specs=[whole(d.shape) for d in diffs]
            + [whole(z_own.shape), pl.BlockSpec((share, wide), lambda i, at: (at[i], 0))],
            out_specs=[whole(one.shape)] * 8,
            scratch_shapes=[pltpu.VMEM((16, toks), BF), pltpu.VMEM((wide, toks), BF)],
        ),
        compiler_params=pltpu.CompilerParams(vmem_limit_bytes=VMEM),
        cost_estimate=pl.CostEstimate(
            flops=2 * toks * sd * wide, bytes_accessed=10 * 2**20, transcendentals=0
        ),
    )(at, *diffs, z_own, projector)


def on_device(attn, out_proj, resid, student, gain, projector):
    toks, wide = resid.shape
    sd = student.shape[1]
    blk = out_proj.shape[1]
    dp, mp = lax.axis_index("dp"), lax.axis_index("mp")
    z, l, c = dp // 4, (dp // 2) % 2, dp % 2
    x, h = mp // 2, mp % 2

    w0 = move(
        out_proj,
        lambda z, l, c, x, h: (z, l, c, x, h) if c == h else (z, l, h, x, 1 - h),
    )

    v = student.astype(F32)
    inv = lax.rsqrt(jnp.mean(v * v, axis=-1, keepdims=True) + 1e-05)
    gain_f = gain.astype(F32)
    normed = (v * inv * gain_f).astype(BF)
    z_own = dot(normed, projector, ((1,), (0,)))
    d0 = (z_own - resid.astype(F32)).astype(BF)
    d0 = jnp.stack([d0[:, q * blk:(q + 1) * blk] for q in range(4)])

    ring, pair, outs = {}, {}, []

    def swap(*slots):
        for s in slots:
            pair[s] = flip(ring[s], e=1)

    def multiply(*slots):
        place = [c ^ h]
        for s in slots:
            to = (z + s) % NZ
            place += [(to // 2 - x) % NX, (to % 2) ^ h]
        blocks = [w for s in slots for w in (ring[s], pair[s])]
        return products(jnp.stack(place).astype(jnp.int32), outs, [attn, a_h, a_l, a_lh], blocks)

    ring[0], attn = gate(w0, attn)
    ring[1], ring[-1] = shift(ring[0], s=-1), shift(ring[0], s=1)
    a_l, a_lh = flip(attn, a=1), flip(attn, a=1, b=1)

    ring, d0 = gate(ring, d0)
    ring[2], ring[-2] = shift(ring[1], s=-1), shift(ring[-1], s=1)
    swap(0)

    ring, pair, attn, a_l, a_lh, normed, d0 = gate(ring, pair, attn, a_l, a_lh, normed, d0)
    ring[3], ring[-3] = shift(ring[2], s=-1), shift(ring[-2], s=1)
    a_h = flip(attn, b=1)
    swap(1, -1)

    ring, pair, normed, d0 = gate(ring, pair, normed, d0)
    d0_t = lax.all_to_all(d0, ("dp", "mp"), 0, 0, axis_index_groups=SQUARES, tiled=True)
    ring[4] = shift(ring[3], s=-1)
    swap(2, -2, 3, -3)
    outs = multiply(0, 1, -1)
    outs = multiply(2, -2)

    ring, pair, outs, d0_t = gate(ring, pair, outs, d0_t)
    swap(4)
    outs = multiply(3, -3)
    outs = multiply(4)

    outs, normed, d0_t = gate(outs, normed, d0_t)
    sums = [shift(outs[k], k=k) if k else outs[k] for k in range(NX)]
    lots = flip(normed[:toks // 2], a=1), flip(normed[toks // 2:], a=1, b=1)
    normed_c = flip(normed, e=1)
    sums, lots, normed_c, normed = gate(sums, lots, normed_c, normed)
    lots_c = [flip(m, e=1) for m in lots]
    stay, leave, *diff_t = difference(
        jnp.stack([l, h, c]).astype(jnp.int32),
        [m.reshape(4, toks, blk) for m in sums],
        d0_t,
    )
    diff_t = {(a, b): diff_t[2 * b + a] for a in range(2) for b in range(2)}

    came = flip(leave, e=1)
    diff_t = {(a, b): flip(diff_t[a, b], a=a, b=b) for a in range(2) for b in range(2)}
    came, lots_c, diff_t = gate(came, lots_c, diff_t)

    rows = sd // NZ
    own = dot(jnp.concatenate([normed, normed_c], 0), jnp.concatenate([stay[0], came[0]], 0), ((0,), (0,)))
    far = dot(jnp.concatenate([*lots, *lots_c], 0), jnp.concatenate([stay[1], came[1]], 0), ((0,), (0,)))
    term = ((own + far) * (1.0 / math.sqrt(toks * NZ * 4))).astype(BF).reshape(NZ, rows, blk)

    terms = lax.all_to_all(term, "dp", 0, 0, axis_index_groups=RINGS, tiled=True)
    grad = jnp.sum(terms.astype(F32), axis=0)
    grad_proj = jnp.zeros((rows // 4, wide), F32)
    for a in range(2):
        for e in range(2):
            p = piece(grad, 2 * (l ^ a) + (h ^ e), rows // 4, 0)
            p = move(p, lambda z, l, c, x, h: (z, l ^ a, h ^ e, x, c))
            grad_proj = put(grad_proj, p, 2 * (l ^ a) + (c ^ e), 1)

    diff, order = [], []
    for b in range(2):
        for a in range(2):
            diff.append(diff_t[a, b])
            order.append(2 * (l ^ a) + (h ^ b))
    share = sd // (NX * 2)
    to = [2 * ((x + k) % NX) + (h ^ b) for k in range(NX) for b in range(2)]
    parts = backs(jnp.stack(to + order).astype(jnp.int32), diff, z_own, projector, share)
    back = parts[0].astype(F32)
    for i in (5, 4, 3, 7, 2, 6, 1):
        back = back + shift(parts[i], k=i // 2, b=i % 2).astype(F32)
    stat = (back[share] + back[share + 1])[:, None]
    xhat = piece(student, mp, share, 1).astype(F32) * inv
    dxhat = back[:share].T * piece(gain_f, mp, share, 0)
    return grad_proj, (inv * (dxhat - xhat * stat)).astype(BF)


def solution(mesh):
    in_specs = (P("dp", "mp"), P("mp", "dp"), P("dp", "mp"), P("dp", None), P(), P(None, "mp"))
    out_specs = (P("dp", "mp"), P("dp", "mp"))
    return jax.shard_map(
        on_device, mesh=mesh, in_specs=in_specs, out_specs=out_specs, check_vma=False
    )
```

```python
import functools
import math

import jax
import jax.numpy as jnp
from jax import lax
from jax.experimental import pallas as pl
from jax.experimental.pallas import tpu as pltpu
from jax.sharding import PartitionSpec as P

NZ, NX = 8, 4
VMEM = 56 * 2**20
BF, F32 = jnp.bfloat16, jnp.float32


def flat(z, l, c, x, h):
    return ((z * 2 + l) * 2 + c) * (NX * 2) + x * 2 + h


PLACES = [
    (z, l, c, x, h)
    for z in range(NZ)
    for l in range(2)
    for c in range(2)
    for x in range(NX)
    for h in range(2)
]


RINGS = [[z * 4 + i for z in range(NZ)] for i in range(4)]
LINES = [[x * 2 + h for x in range(NX)] for h in range(2)]
SQUARES = [
    [flat(z, l, c, x, h) for l in range(2) for h in range(2)]
    for z in range(NZ)
    for c in range(2)
    for x in range(NX)
]


def move(value, to):
    return lax.ppermute(value, ("dp", "mp"), [(flat(*p), flat(*to(*p))) for p in PLACES])


def flip(value, a=0, b=0, e=0):
    if not a + b + e:
        return value
    return move(value, lambda z, l, c, x, h: (z, l ^ a, c ^ e, x, h ^ b))


def shift(value, s=0, k=0, b=0):
    return move(value, lambda z, l, c, x, h: ((z + s) % NZ, l, c, (x + k) % NX, h ^ b))


def after(value, *first):
    return lax.optimization_barrier((value, *first))[0]


def gate(*values):
    return lax.optimization_barrier(values)


def dot(a, b, dims):
    return lax.dot_general(a, b, (dims, ((), ())), preferred_element_type=F32)


def piece(value, index, size, axis):
    return lax.dynamic_slice_in_dim(value, index * size, size, axis)


def put(whole, value, index, axis):
    return lax.dynamic_update_slice_in_dim(whole, value, index * value.shape[axis], axis)


def difference_kernel(at, m0, m1, m2, m3, d0, stay, leave, *pieces):
    l, h, c = at[0], at[1], at[2]
    for b in range(2):
        for a in range(2):
            own = 2 * b + a
            total = m0[own].astype(F32) + m1[own].astype(F32) + m2[own].astype(F32) + m3[own].astype(F32)
            diff = (d0[2 * (l ^ a) + (h ^ b)].astype(F32) - total).astype(BF)
            pieces[2 * b + a][...] = diff

            @pl.when((h ^ b) == c)
            def _():
                stay[a] = diff

            @pl.when((h ^ b) != c)
            def _():
                leave[a] = diff


def difference(at, sums, d0):
    one = jax.ShapeDtypeStruct(d0.shape[1:], BF)
    two = jax.ShapeDtypeStruct((2, *d0.shape[1:]), BF)
    return pl.pallas_call(
        difference_kernel,
        out_shape=[two, two, one, one, one, one],
        grid=(1,),
        in_specs=[pl.BlockSpec(memory_space=pltpu.SMEM)] + [whole(d0.shape)] * 5,
        out_specs=[whole(two.shape)] * 2 + [whole(one.shape)] * 4,
        compiler_params=pltpu.CompilerParams(vmem_limit_bytes=VMEM),
    )(at, *sums, d0)


def whole(shape):
    return pl.BlockSpec(shape, lambda *i: (0,) * len(shape))


def products_kernel(n, kept, at, *refs):
    attn, a_h, a_l, a_lh = refs[kept:kept + 4]
    blocks = refs[kept + 4:kept + 4 + 2 * n]
    outs, (made, sems) = refs[kept + 4 + 2 * n:-2], refs[-2:]
    toks = attn.shape[0]

    def run(turn):
        for i in range(n):
            w_h, w_o = blocks[2 * i + turn], blocks[2 * i + 1 - turn]
            for a, (near, far) in enumerate(((attn, a_h), (a_l, a_lh))):
                part = jnp.dot(near[...], w_h[...], preferred_element_type=F32)
                part = part + jnp.dot(far[...], w_o[...], preferred_element_type=F32)
                made[i, a * toks:(a + 1) * toks] = part.astype(BF)

    pl.when(at[0] == 0)(lambda: run(0))
    pl.when(at[0] != 0)(lambda: run(1))
    for i in range(n):
        for k in range(NX):

            @pl.when(at[1 + 2 * i] == k)
            def _():
                copy = pltpu.make_async_copy(made.at[i], outs[k].at[at[2 + 2 * i]], sems.at[i])
                copy.start()
                copy.wait()


def products(at, kept, heads, blocks):
    n = len(blocks) // 2
    toks, blk = heads[0].shape[0], blocks[0].shape[1]
    anywhere = pl.BlockSpec(memory_space=pl.ANY)
    return pl.pallas_call(
        functools.partial(products_kernel, n, len(kept)),
        out_shape=[jax.ShapeDtypeStruct((2, 2 * toks, blk), BF)] * NX,
        grid=(1,),
        in_specs=[pl.BlockSpec(memory_space=pltpu.SMEM)]
        + [anywhere] * len(kept)
        + [whole(m.shape) for m in (*heads, *blocks)],
        out_specs=[anywhere] * NX,
        scratch_shapes=[pltpu.VMEM((n, 2 * toks, blk), BF), pltpu.SemaphoreType.DMA((n,))],
        input_output_aliases={1 + k: k for k in range(len(kept))},
        compiler_params=pltpu.CompilerParams(vmem_limit_bytes=VMEM),
        cost_estimate=pl.CostEstimate(
            flops=n * 8 * toks * blk * heads[0].shape[1], bytes_accessed=8 * 2**20, transcendentals=0
        ),
    )(at, *kept, *heads, *blocks)


def back_kernel(sd, at, d0, d1, d2, d3, z_own, rows_p, *refs):
    outs, (tail, turned) = refs[:-2], refs[-2:]
    share = rows_p.shape[0]
    step = pl.program_id(0)
    toks, blk = d0.shape
    columns = [pl.ds(pl.multiple_of(at[8 + q] * blk, blk), blk) for q in range(4)]
    pieces = (d0, d1, d2, d3)

    @pl.when(step == 0)
    def _():
        stat = 0.0
        for d, q in zip(pieces, columns):
            turned[q] = d[...].astype(F32).T.astype(BF)
            stat = stat + jnp.sum(d[...].astype(F32) * z_own[:, q], axis=-1, keepdims=True)
        stat = jnp.broadcast_to(stat / sd, (toks, 128)).T[:16]
        high = stat.astype(BF)
        low = (stat - high.astype(F32)).astype(BF)
        row = lax.broadcasted_iota(jnp.int32, stat.shape, 0)
        kept = jnp.where(row == 0, high.astype(F32), jnp.where(row == 1, low.astype(F32), 0.0))
        tail[...] = kept.astype(BF)

    part = jnp.dot(rows_p[...], turned[...], preferred_element_type=F32)
    for k, out in enumerate(outs):

        @pl.when(step == k)
        def _():
            out[:share] = part.astype(BF)
            out[share:] = tail[...]


def backs(at, diffs, z_own, projector, share):
    toks, blk = diffs[0].shape
    sd, wide = projector.shape
    one = jax.ShapeDtypeStruct((share + 16, toks), BF)
    return pl.pallas_call(
        functools.partial(back_kernel, sd),
        out_shape=[one] * 8,
        grid_spec=pltpu.PrefetchScalarGridSpec(
            num_scalar_prefetch=1,
            grid=(8,),
            in_specs=[whole(d.shape) for d in diffs]
            + [whole(z_own.shape), pl.BlockSpec((share, wide), lambda i, at: (at[i], 0))],
            out_specs=[whole(one.shape)] * 8,
            scratch_shapes=[pltpu.VMEM((16, toks), BF), pltpu.VMEM((wide, toks), BF)],
        ),
        compiler_params=pltpu.CompilerParams(vmem_limit_bytes=VMEM),
        cost_estimate=pl.CostEstimate(
            flops=2 * toks * sd * wide, bytes_accessed=10 * 2**20, transcendentals=0
        ),
    )(at, *diffs, z_own, projector)


def on_device(attn, out_proj, resid, student, gain, projector):
    toks, wide = resid.shape
    sd = student.shape[1]
    blk = out_proj.shape[1]
    dp, mp = lax.axis_index("dp"), lax.axis_index("mp")
    z, l, c = dp // 4, (dp // 2) % 2, dp % 2
    x, h = mp // 2, mp % 2

    w0 = move(
        out_proj,
        lambda z, l, c, x, h: (z, l, c, x, h) if c == h else (z, l, h, x, 1 - h),
    )

    v = student.astype(F32)
    inv = lax.rsqrt(jnp.mean(v * v, axis=-1, keepdims=True) + 1e-05)
    gain_f = gain.astype(F32)
    normed = (v * inv * gain_f).astype(BF)
    z_own = dot(normed, projector, ((1,), (0,)))
    d0 = (z_own - resid.astype(F32)).astype(BF)
    d0 = jnp.stack([d0[:, q * blk:(q + 1) * blk] for q in range(4)])

    ring, pair, outs = {}, {}, []

    def swap(*slots):
        for s in slots:
            pair[s] = flip(ring[s], e=1)

    def multiply(*slots):
        place = [c ^ h]
        for s in slots:
            to = (z + s) % NZ
            place += [(to // 2 - x) % NX, (to % 2) ^ h]
        blocks = [w for s in slots for w in (ring[s], pair[s])]
        return products(jnp.stack(place).astype(jnp.int32), outs, [attn, a_h, a_l, a_lh], blocks)

    ring[0], attn = gate(w0, attn)
    ring[1], ring[-1] = shift(ring[0], s=-1), shift(ring[0], s=1)
    a_l, a_lh = flip(attn, a=1), flip(attn, a=1, b=1)
    swap(0)

    ring, d0, normed = gate(ring, d0, normed)
    ring[2], ring[-2] = shift(ring[1], s=-1), shift(ring[-1], s=1)
    normed_c = flip(normed, e=1)

    ring, pair, attn, a_l, a_lh, normed, normed_c, d0 = gate(ring, pair, attn, a_l, a_lh, normed, normed_c, d0)
    ring[3], ring[-3] = shift(ring[2], s=-1), shift(ring[-2], s=1)
    a_h = flip(attn, b=1)
    swap(1, -1)

    ring, pair, normed, d0 = gate(ring, pair, normed, d0)
    ring[4] = shift(ring[3], s=-1)
    swap(2, -2, 3, -3)
    outs = multiply(0, 1, -1)
    outs = multiply(2, -2, 3, -3)

    ring, outs = gate(ring, outs)
    swap(4)
    outs = multiply(4)

    outs, normed, d0 = gate(outs, normed, d0)
    sums = [shift(outs[k], k=k) if k else outs[k] for k in range(NX)]
    lots = flip(normed[:toks // 2], a=1), flip(normed[toks // 2:], a=1, b=1)
    d0_t = lax.all_to_all(d0, ("dp", "mp"), 0, 0, axis_index_groups=SQUARES, tiled=True)
    sums, lots, d0_t = gate(sums, lots, d0_t)
    stay, leave, *diff_t = difference(
        jnp.stack([l, h, c]).astype(jnp.int32),
        [m.reshape(4, toks, blk) for m in sums],
        d0_t,
    )
    diff_t = {(a, b): diff_t[2 * b + a] for a in range(2) for b in range(2)}

    came = flip(leave, e=1)
    diff_t = {(a, b): flip(diff_t[a, b], a=a, b=b) for a in range(2) for b in range(2)}
    lots, came = gate(lots, came)
    lots_c = [flip(m, e=1) for m in lots]

    rows = sd // NZ
    own = dot(jnp.concatenate([normed, normed_c], 0), jnp.concatenate([stay[0], came[0]], 0), ((0,), (0,)))
    far = dot(jnp.concatenate([*lots, *lots_c], 0), jnp.concatenate([stay[1], came[1]], 0), ((0,), (0,)))
    own, far, diff_t = gate(own, far, diff_t)
    term = ((own + far) * (1.0 / math.sqrt(toks * NZ * 4))).astype(BF).reshape(NZ, rows, blk)

    terms = lax.all_to_all(term, "dp", 0, 0, axis_index_groups=RINGS, tiled=True)
    grad = jnp.sum(terms.astype(F32), axis=0)
    grad_proj = jnp.zeros((rows // 4, wide), F32)
    for a in range(2):
        for e in range(2):
            p = piece(grad, 2 * (l ^ a) + (h ^ e), rows // 4, 0)
            p = move(p, lambda z, l, c, x, h: (z, l ^ a, h ^ e, x, c))
            grad_proj = put(grad_proj, p, 2 * (l ^ a) + (c ^ e), 1)

    diff, order = [], []
    for b in range(2):
        for a in range(2):
            diff.append(diff_t[a, b])
            order.append(2 * (l ^ a) + (h ^ b))
    share = sd // (NX * 2)
    to = [2 * ((x + k) % NX) + (h ^ b) for k in range(NX) for b in range(2)]
    parts = backs(jnp.stack(to + order).astype(jnp.int32), diff, z_own, projector, share)
    back = parts[0].astype(F32)
    for i in (5, 4, 3, 7, 2, 6, 1):
        back = back + shift(parts[i], k=i // 2, b=i % 2).astype(F32)
    stat = (back[share] + back[share + 1])[:, None]
    xhat = piece(student, mp, share, 1).astype(F32) * inv
    dxhat = back[:share].T * piece(gain_f, mp, share, 0)
    return grad_proj, (inv * (dxhat - xhat * stat)).astype(BF)


def solution(mesh):
    in_specs = (P("dp", "mp"), P("mp", "dp"), P("dp", "mp"), P("dp", None), P(), P(None, "mp"))
    out_specs = (P("dp", "mp"), P("dp", "mp"))
    return jax.shard_map(
        on_device, mesh=mesh, in_specs=in_specs, out_specs=out_specs, check_vma=False
    )
```

```python
import functools
import math

import jax
import jax.numpy as jnp
from jax import lax
from jax.experimental import pallas as pl
from jax.experimental.pallas import tpu as pltpu
from jax.sharding import PartitionSpec as P

NZ, NX = 8, 4
VMEM = 56 * 2**20
BF, F32 = jnp.bfloat16, jnp.float32


def flat(z, l, c, x, h):
    return ((z * 2 + l) * 2 + c) * (NX * 2) + x * 2 + h


PLACES = [
    (z, l, c, x, h)
    for z in range(NZ)
    for l in range(2)
    for c in range(2)
    for x in range(NX)
    for h in range(2)
]


RINGS = [[z * 4 + i for z in range(NZ)] for i in range(4)]
LINES = [[x * 2 + h for x in range(NX)] for h in range(2)]
SQUARES = [
    [flat(z, l, c, x, h) for l in range(2) for h in range(2)]
    for z in range(NZ)
    for c in range(2)
    for x in range(NX)
]


def move(value, to):
    return lax.ppermute(value, ("dp", "mp"), [(flat(*p), flat(*to(*p))) for p in PLACES])


def flip(value, a=0, b=0, e=0):
    if not a + b + e:
        return value
    return move(value, lambda z, l, c, x, h: (z, l ^ a, c ^ e, x, h ^ b))


def shift(value, s=0, k=0, b=0):
    return move(value, lambda z, l, c, x, h: ((z + s) % NZ, l, c, (x + k) % NX, h ^ b))


def after(value, *first):
    return lax.optimization_barrier((value, *first))[0]


def gate(*values):
    return lax.optimization_barrier(values)


def dot(a, b, dims):
    return lax.dot_general(a, b, (dims, ((), ())), preferred_element_type=F32)


def piece(value, index, size, axis):
    return lax.dynamic_slice_in_dim(value, index * size, size, axis)


def put(whole, value, index, axis):
    return lax.dynamic_update_slice_in_dim(whole, value, index * value.shape[axis], axis)


def difference_kernel(at, m0, m1, m2, m3, d0, stay, leave, *pieces):
    l, h, c = at[0], at[1], at[2]
    for b in range(2):
        for a in range(2):
            own = 2 * b + a
            total = m0[own].astype(F32) + m1[own].astype(F32) + m2[own].astype(F32) + m3[own].astype(F32)
            diff = (d0[2 * (l ^ a) + (h ^ b)].astype(F32) - total).astype(BF)
            pieces[2 * b + a][...] = diff

            @pl.when((h ^ b) == c)
            def _():
                stay[a] = diff

            @pl.when((h ^ b) != c)
            def _():
                leave[a] = diff


def difference(at, sums, d0):
    one = jax.ShapeDtypeStruct(d0.shape[1:], BF)
    two = jax.ShapeDtypeStruct((2, *d0.shape[1:]), BF)
    return pl.pallas_call(
        difference_kernel,
        out_shape=[two, two, one, one, one, one],
        grid=(1,),
        in_specs=[pl.BlockSpec(memory_space=pltpu.SMEM)] + [whole(d0.shape)] * 5,
        out_specs=[whole(two.shape)] * 2 + [whole(one.shape)] * 4,
        compiler_params=pltpu.CompilerParams(vmem_limit_bytes=VMEM),
    )(at, *sums, d0)


def whole(shape):
    return pl.BlockSpec(shape, lambda *i: (0,) * len(shape))


def products_kernel(n, kept, at, *refs):
    attn, a_h, a_l, a_lh = refs[kept:kept + 4]
    blocks = refs[kept + 4:kept + 4 + 2 * n]
    outs, (made, sems) = refs[kept + 4 + 2 * n:-2], refs[-2:]
    toks = attn.shape[0]

    def run(turn):
        for i in range(n):
            w_h, w_o = blocks[2 * i + turn], blocks[2 * i + 1 - turn]
            for a, (near, far) in enumerate(((attn, a_h), (a_l, a_lh))):
                part = jnp.dot(near[...], w_h[...], preferred_element_type=F32)
                part = part + jnp.dot(far[...], w_o[...], preferred_element_type=F32)
                made[i, a * toks:(a + 1) * toks] = part.astype(BF)

    pl.when(at[0] == 0)(lambda: run(0))
    pl.when(at[0] != 0)(lambda: run(1))
    for i in range(n):
        for k in range(NX):

            @pl.when(at[1 + 2 * i] == k)
            def _():
                copy = pltpu.make_async_copy(made.at[i], outs[k].at[at[2 + 2 * i]], sems.at[i])
                copy.start()
                copy.wait()


def products(at, kept, heads, blocks):
    n = len(blocks) // 2
    toks, blk = heads[0].shape[0], blocks[0].shape[1]
    anywhere = pl.BlockSpec(memory_space=pl.ANY)
    return pl.pallas_call(
        functools.partial(products_kernel, n, len(kept)),
        out_shape=[jax.ShapeDtypeStruct((2, 2 * toks, blk), BF)] * NX,
        grid=(1,),
        in_specs=[pl.BlockSpec(memory_space=pltpu.SMEM)]
        + [anywhere] * len(kept)
        + [whole(m.shape) for m in (*heads, *blocks)],
        out_specs=[anywhere] * NX,
        scratch_shapes=[pltpu.VMEM((n, 2 * toks, blk), BF), pltpu.SemaphoreType.DMA((n,))],
        input_output_aliases={1 + k: k for k in range(len(kept))},
        compiler_params=pltpu.CompilerParams(vmem_limit_bytes=VMEM),
        cost_estimate=pl.CostEstimate(
            flops=n * 8 * toks * blk * heads[0].shape[1], bytes_accessed=8 * 2**20, transcendentals=0
        ),
    )(at, *kept, *heads, *blocks)


def back_kernel(sd, at, d0, d1, d2, d3, z_own, rows_p, *refs):
    outs, (tail, turned) = refs[:-2], refs[-2:]
    share = rows_p.shape[0] // 2
    step = pl.program_id(0)
    toks, blk = d0.shape
    columns = [pl.ds(pl.multiple_of(at[8 + q] * blk, blk), blk) for q in range(4)]
    pieces = (d0, d1, d2, d3)

    @pl.when(step == 0)
    def _():
        stat = 0.0
        for d, q in zip(pieces, columns):
            turned[q] = d[...].astype(F32).T.astype(BF)
            stat = stat + jnp.sum(d[...].astype(F32) * z_own[:, q], axis=-1, keepdims=True)
        stat = jnp.broadcast_to(stat / sd, (toks, 128)).T[:16]
        high = stat.astype(BF)
        low = (stat - high.astype(F32)).astype(BF)
        row = lax.broadcasted_iota(jnp.int32, stat.shape, 0)
        kept = jnp.where(row == 0, high.astype(F32), jnp.where(row == 1, low.astype(F32), 0.0))
        tail[...] = kept.astype(BF)

    part = jnp.dot(rows_p[...], turned[...], preferred_element_type=F32)
    near, far = part[:share], part[share:]
    halves = jnp.where(at[4] == 0, near, far), jnp.where(at[4] == 0, far, near)
    for k, out in enumerate(outs):

        @pl.when(step == k // 2)
        def _():
            out[:share] = halves[k % 2].astype(BF)
            out[share:] = tail[...]


def backs(at, diffs, z_own, projector, share):
    toks, blk = diffs[0].shape
    sd, wide = projector.shape
    one = jax.ShapeDtypeStruct((share + 16, toks), BF)
    return pl.pallas_call(
        functools.partial(back_kernel, sd),
        out_shape=[one] * 8,
        grid_spec=pltpu.PrefetchScalarGridSpec(
            num_scalar_prefetch=1,
            grid=(NX,),
            in_specs=[whole(d.shape) for d in diffs]
            + [whole(z_own.shape), pl.BlockSpec((2 * share, wide), lambda i, at: (at[i], 0))],
            out_specs=[whole(one.shape)] * 8,
            scratch_shapes=[pltpu.VMEM((16, toks), BF), pltpu.VMEM((wide, toks), BF)],
        ),
        compiler_params=pltpu.CompilerParams(vmem_limit_bytes=VMEM),
        cost_estimate=pl.CostEstimate(
            flops=2 * toks * sd * wide, bytes_accessed=10 * 2**20, transcendentals=0
        ),
    )(at, *diffs, z_own, projector)


def on_device(attn, out_proj, resid, student, gain, projector):
    toks, wide = resid.shape
    sd = student.shape[1]
    blk = out_proj.shape[1]
    dp, mp = lax.axis_index("dp"), lax.axis_index("mp")
    z, l, c = dp // 4, (dp // 2) % 2, dp % 2
    x, h = mp // 2, mp % 2

    w0 = move(
        out_proj,
        lambda z, l, c, x, h: (z, l, c, x, h) if c == h else (z, l, h, x, 1 - h),
    )

    v = student.astype(F32)
    inv = lax.rsqrt(jnp.mean(v * v, axis=-1, keepdims=True) + 1e-05)
    gain_f = gain.astype(F32)
    normed = (v * inv * gain_f).astype(BF)

    ring, pair, outs = {}, {}, []

    def swap(*slots):
        for s in slots:
            pair[s] = flip(ring[s], e=1)

    def multiply(*slots):
        place = [c ^ h]
        for s in slots:
            to = (z + s) % NZ
            place += [(to // 2 - x) % NX, (to % 2) ^ h]
        blocks = [w for s in slots for w in (ring[s], pair[s])]
        return products(jnp.stack(place).astype(jnp.int32), outs, [attn, a_h, a_l, a_lh], blocks)

    ring[0], attn = gate(w0, attn)
    ring[1], ring[-1] = shift(ring[0], s=-1), shift(ring[0], s=1)
    a_l, a_lh = flip(attn, a=1), flip(attn, a=1, b=1)

    ring, normed = gate(ring, normed)
    ring[2], ring[-2] = shift(ring[1], s=-1), shift(ring[-1], s=1)
    swap(0)
    z_own = dot(normed, projector, ((1,), (0,)))
    d0 = (z_own - resid.astype(F32)).astype(BF)
    d0 = jnp.stack([d0[:, q * blk:(q + 1) * blk] for q in range(4)])

    ring, pair, attn, a_l, a_lh, normed, d0, z_own = gate(ring, pair, attn, a_l, a_lh, normed, d0, z_own)
    ring[3], ring[-3] = shift(ring[2], s=-1), shift(ring[-2], s=1)
    a_h = flip(attn, b=1)
    swap(1, -1)

    ring, pair, normed, d0 = gate(ring, pair, normed, d0)
    ring[4] = shift(ring[3], s=-1)
    swap(2, -2, 3, -3)
    normed_c = flip(normed, e=1)
    outs = multiply(0, 1, -1)
    outs = multiply(2, -2, 3, -3)

    ring, outs, normed_c = gate(ring, outs, normed_c)
    swap(4)
    outs = multiply(4)

    outs, normed, d0 = gate(outs, normed, d0)
    sums = [shift(outs[k], k=k) if k else outs[k] for k in range(NX)]
    lots = flip(normed[:toks // 2], a=1), flip(normed[toks // 2:], a=1, b=1)
    d0_t = lax.all_to_all(d0, ("dp", "mp"), 0, 0, axis_index_groups=SQUARES, tiled=True)
    sums, lots, d0_t = gate(sums, lots, d0_t)
    stay, leave, *diff_t = difference(
        jnp.stack([l, h, c]).astype(jnp.int32),
        [m.reshape(4, toks, blk) for m in sums],
        d0_t,
    )
    diff_t = {(a, b): diff_t[2 * b + a] for a in range(2) for b in range(2)}

    came = flip(leave, e=1)
    diff_t = {(a, b): flip(diff_t[a, b], a=a, b=b) for a in range(2) for b in range(2)}
    lots, came = gate(lots, came)
    lots_c = [flip(m, e=1) for m in lots]

    rows = sd // NZ
    own = dot(jnp.concatenate([normed, normed_c], 0), jnp.concatenate([stay[0], came[0]], 0), ((0,), (0,)))
    far = dot(jnp.concatenate([*lots, *lots_c], 0), jnp.concatenate([stay[1], came[1]], 0), ((0,), (0,)))
    own, far, diff_t = gate(own, far, diff_t)
    term = ((own + far) * (1.0 / math.sqrt(toks * NZ * 4))).astype(BF).reshape(NZ, rows, blk)

    terms = lax.all_to_all(term, "dp", 0, 0, axis_index_groups=RINGS, tiled=True)
    grad = jnp.sum(terms.astype(F32), axis=0)
    grad_proj = jnp.zeros((rows // 4, wide), F32)
    for a in range(2):
        for e in range(2):
            p = piece(grad, 2 * (l ^ a) + (h ^ e), rows // 4, 0)
            p = move(p, lambda z, l, c, x, h: (z, l ^ a, h ^ e, x, c))
            grad_proj = put(grad_proj, p, 2 * (l ^ a) + (c ^ e), 1)

    diff, order = [], []
    for b in range(2):
        for a in range(2):
            diff.append(diff_t[a, b])
            order.append(2 * (l ^ a) + (h ^ b))
    share = sd // (NX * 2)
    to = [(x + k) % NX for k in range(NX)] + [h] * 4
    parts = backs(jnp.stack(to + order).astype(jnp.int32), diff, z_own, projector, share)
    back = parts[0].astype(F32)
    for i in (5, 4, 3, 7, 2, 6, 1):
        back = back + shift(parts[i], k=i // 2, b=i % 2).astype(F32)
    stat = (back[share] + back[share + 1])[:, None]
    xhat = piece(student, mp, share, 1).astype(F32) * inv
    dxhat = back[:share].T * piece(gain_f, mp, share, 0)
    return grad_proj, (inv * (dxhat - xhat * stat)).astype(BF)


def solution(mesh):
    in_specs = (P("dp", "mp"), P("mp", "dp"), P("dp", "mp"), P("dp", None), P(), P(None, "mp"))
    out_specs = (P("dp", "mp"), P("dp", "mp"))
    return jax.shard_map(
        on_device, mesh=mesh, in_specs=in_specs, out_specs=out_specs, check_vma=False
    )
```

```python
import functools
import math

import jax
import jax.numpy as jnp
from jax import lax
from jax.experimental import pallas as pl
from jax.experimental.pallas import tpu as pltpu
from jax.sharding import PartitionSpec as P

NZ, NX = 8, 4
VMEM = 56 * 2**20
BF, F32 = jnp.bfloat16, jnp.float32


def flat(z, l, c, x, h):
    return ((z * 2 + l) * 2 + c) * (NX * 2) + x * 2 + h


PLACES = [
    (z, l, c, x, h)
    for z in range(NZ)
    for l in range(2)
    for c in range(2)
    for x in range(NX)
    for h in range(2)
]


RINGS = [[z * 4 + i for z in range(NZ)] for i in range(4)]
LINES = [[x * 2 + h for x in range(NX)] for h in range(2)]
SQUARES = [
    [flat(z, l, c, x, h) for l in range(2) for h in range(2)]
    for z in range(NZ)
    for c in range(2)
    for x in range(NX)
]


def move(value, to):
    return lax.ppermute(value, ("dp", "mp"), [(flat(*p), flat(*to(*p))) for p in PLACES])


def flip(value, a=0, b=0, e=0):
    if not a + b + e:
        return value
    return move(value, lambda z, l, c, x, h: (z, l ^ a, c ^ e, x, h ^ b))


def shift(value, s=0, k=0, b=0):
    return move(value, lambda z, l, c, x, h: ((z + s) % NZ, l, c, (x + k) % NX, h ^ b))


def after(value, *first):
    return lax.optimization_barrier((value, *first))[0]


def gate(*values):
    return lax.optimization_barrier(values)


def dot(a, b, dims):
    return lax.dot_general(a, b, (dims, ((), ())), preferred_element_type=F32)


def piece(value, index, size, axis):
    return lax.dynamic_slice_in_dim(value, index * size, size, axis)


def put(whole, value, index, axis):
    return lax.dynamic_update_slice_in_dim(whole, value, index * value.shape[axis], axis)


def difference_kernel(at, m0, m1, m2, m3, d0, stay, leave, *pieces):
    l, h, c = at[0], at[1], at[2]
    for b in range(2):
        for a in range(2):
            own = 2 * b + a
            total = m0[own].astype(F32) + m1[own].astype(F32) + m2[own].astype(F32) + m3[own].astype(F32)
            diff = (d0[2 * (l ^ a) + (h ^ b)].astype(F32) - total).astype(BF)
            pieces[2 * b + a][...] = diff

            @pl.when((h ^ b) == c)
            def _():
                stay[a] = diff

            @pl.when((h ^ b) != c)
            def _():
                leave[a] = diff


def difference(at, sums, d0):
    one = jax.ShapeDtypeStruct(d0.shape[1:], BF)
    two = jax.ShapeDtypeStruct((2, *d0.shape[1:]), BF)
    return pl.pallas_call(
        difference_kernel,
        out_shape=[two, two, one, one, one, one],
        grid=(1,),
        in_specs=[pl.BlockSpec(memory_space=pltpu.SMEM)] + [whole(d0.shape)] * 5,
        out_specs=[whole(two.shape)] * 2 + [whole(one.shape)] * 4,
        compiler_params=pltpu.CompilerParams(vmem_limit_bytes=VMEM),
    )(at, *sums, d0)


def whole(shape):
    return pl.BlockSpec(shape, lambda *i: (0,) * len(shape))


def products_kernel(n, kept, at, *refs):
    attn, a_h, a_l, a_lh = refs[kept:kept + 4]
    blocks = refs[kept + 4:kept + 4 + 2 * n]
    outs, (made, sems) = refs[kept + 4 + 2 * n:-2], refs[-2:]
    toks = attn.shape[0]

    def run(turn):
        for i in range(n):
            w_h, w_o = blocks[2 * i + turn], blocks[2 * i + 1 - turn]
            for a, (near, far) in enumerate(((attn, a_h), (a_l, a_lh))):
                part = jnp.dot(near[...], w_h[...], preferred_element_type=F32)
                part = part + jnp.dot(far[...], w_o[...], preferred_element_type=F32)
                made[i, a * toks:(a + 1) * toks] = part.astype(BF)

    pl.when(at[0] == 0)(lambda: run(0))
    pl.when(at[0] != 0)(lambda: run(1))
    for i in range(n):
        for k in range(NX):

            @pl.when(at[1 + 2 * i] == k)
            def _():
                copy = pltpu.make_async_copy(made.at[i], outs[k].at[at[2 + 2 * i]], sems.at[i])
                copy.start()
                copy.wait()


def products(at, kept, heads, blocks):
    n = len(blocks) // 2
    toks, blk = heads[0].shape[0], blocks[0].shape[1]
    anywhere = pl.BlockSpec(memory_space=pl.ANY)
    return pl.pallas_call(
        functools.partial(products_kernel, n, len(kept)),
        out_shape=[jax.ShapeDtypeStruct((2, 2 * toks, blk), BF)] * NX,
        grid=(1,),
        in_specs=[pl.BlockSpec(memory_space=pltpu.SMEM)]
        + [anywhere] * len(kept)
        + [whole(m.shape) for m in (*heads, *blocks)],
        out_specs=[anywhere] * NX,
        scratch_shapes=[pltpu.VMEM((n, 2 * toks, blk), BF), pltpu.SemaphoreType.DMA((n,))],
        input_output_aliases={1 + k: k for k in range(len(kept))},
        compiler_params=pltpu.CompilerParams(vmem_limit_bytes=VMEM),
        cost_estimate=pl.CostEstimate(
            flops=n * 8 * toks * blk * heads[0].shape[1], bytes_accessed=8 * 2**20, transcendentals=0
        ),
    )(at, *kept, *heads, *blocks)


def back_kernel(sd, at, d0, d1, d2, d3, z_own, rows_p, *refs):
    outs, (tail, turned) = refs[:-2], refs[-2:]
    share = rows_p.shape[0] // 2
    step = pl.program_id(0)
    toks, blk = d0.shape
    columns = [pl.ds(pl.multiple_of(at[8 + q] * blk, blk), blk) for q in range(4)]
    pieces = (d0, d1, d2, d3)

    @pl.when(step == 0)
    def _():
        stat = 0.0
        for d, q in zip(pieces, columns):
            turned[q] = d[...].astype(F32).T.astype(BF)
            stat = stat + jnp.sum(d[...].astype(F32) * z_own[:, q], axis=-1, keepdims=True)
        stat = jnp.broadcast_to(stat / sd, (toks, 128)).T[:16]
        high = stat.astype(BF)
        low = (stat - high.astype(F32)).astype(BF)
        row = lax.broadcasted_iota(jnp.int32, stat.shape, 0)
        kept = jnp.where(row == 0, high.astype(F32), jnp.where(row == 1, low.astype(F32), 0.0))
        tail[...] = kept.astype(BF)

    part = jnp.dot(rows_p[...], turned[...], preferred_element_type=F32)
    near, far = part[:share], part[share:]
    halves = jnp.where(at[4] == 0, near, far), jnp.where(at[4] == 0, far, near)
    for k, out in enumerate(outs):

        @pl.when(step == k // 2)
        def _():
            out[:share] = halves[k % 2].astype(BF)
            out[share:] = tail[...]


def backs(at, diffs, z_own, projector, share):
    toks, blk = diffs[0].shape
    sd, wide = projector.shape
    one = jax.ShapeDtypeStruct((share + 16, toks), BF)
    return pl.pallas_call(
        functools.partial(back_kernel, sd),
        out_shape=[one] * 8,
        grid_spec=pltpu.PrefetchScalarGridSpec(
            num_scalar_prefetch=1,
            grid=(NX,),
            in_specs=[whole(d.shape) for d in diffs]
            + [whole(z_own.shape), pl.BlockSpec((2 * share, wide), lambda i, at: (at[i], 0))],
            out_specs=[whole(one.shape)] * 8,
            scratch_shapes=[pltpu.VMEM((16, toks), BF), pltpu.VMEM((wide, toks), BF)],
        ),
        compiler_params=pltpu.CompilerParams(vmem_limit_bytes=VMEM),
        cost_estimate=pl.CostEstimate(
            flops=2 * toks * sd * wide, bytes_accessed=10 * 2**20, transcendentals=0
        ),
    )(at, *diffs, z_own, projector)


def on_device(attn, out_proj, resid, student, gain, projector):
    toks, wide = resid.shape
    sd = student.shape[1]
    blk = out_proj.shape[1]
    dp, mp = lax.axis_index("dp"), lax.axis_index("mp")
    z, l, c = dp // 4, (dp // 2) % 2, dp % 2
    x, h = mp // 2, mp % 2

    w0 = move(
        out_proj,
        lambda z, l, c, x, h: (z, l, c, x, h) if c == h else (z, l, h, x, 1 - h),
    )

    v = student.astype(F32)
    inv = lax.rsqrt(jnp.mean(v * v, axis=-1, keepdims=True) + 1e-05)
    gain_f = gain.astype(F32)
    normed = (v * inv * gain_f).astype(BF)

    ring, pair, outs = {}, {}, []

    def swap(*slots):
        for s in slots:
            pair[s] = flip(ring[s], e=1)

    def multiply(*slots):
        place = [c ^ h]
        for s in slots:
            to = (z + s) % NZ
            place += [(to // 2 - x) % NX, (to % 2) ^ h]
        blocks = [w for s in slots for w in (ring[s], pair[s])]
        return products(jnp.stack(place).astype(jnp.int32), outs, [attn, a_h, a_l, a_lh], blocks)

    ring[0], attn = gate(w0, attn)
    ring[1], ring[-1] = shift(ring[0], s=-1), shift(ring[0], s=1)
    a_l, a_lh = flip(attn, a=1), flip(attn, a=1, b=1)

    ring, normed = gate(ring, normed)
    ring[2], ring[-2] = shift(ring[1], s=-1), shift(ring[-1], s=1)
    swap(0)
    z_own = dot(normed, projector, ((1,), (0,)))
    d0 = (z_own - resid.astype(F32)).astype(BF)
    d0 = jnp.stack([d0[:, q * blk:(q + 1) * blk] for q in range(4)])

    lots = normed[:toks // 2], normed[toks // 2:]

    ring, pair, attn, a_l, a_lh, normed, d0, z_own, lots = gate(ring, pair, attn, a_l, a_lh, normed, d0, z_own, lots)
    ring[3], ring[-3] = shift(ring[2], s=-1), shift(ring[-2], s=1)
    a_h = flip(attn, b=1)
    swap(1, -1)

    ring, pair, normed, d0, a_h = gate(ring, pair, normed, d0, a_h)
    ring[4] = shift(ring[3], s=-1)
    swap(2, -2, 3, -3)
    normed_c = flip(normed, e=1)
    outs = multiply(0, 1, -1)
    outs = multiply(2, -2, 3, -3)

    ring, outs, normed_c = gate(ring, outs, normed_c)
    swap(4)
    outs = multiply(4)

    outs, lots, d0 = gate(outs, lots, d0)
    sums = [shift(outs[k], k=k) if k else outs[k] for k in range(NX)]
    lots = flip(lots[0], a=1), flip(lots[1], a=1, b=1)
    d0_t = lax.all_to_all(d0, ("dp", "mp"), 0, 0, axis_index_groups=SQUARES, tiled=True)
    sums, lots, d0_t = gate(sums, lots, d0_t)
    stay, leave, *diff_t = difference(
        jnp.stack([l, h, c]).astype(jnp.int32),
        [m.reshape(4, toks, blk) for m in sums],
        d0_t,
    )
    diff_t = {(a, b): diff_t[2 * b + a] for a in range(2) for b in range(2)}

    came = flip(leave, e=1)
    diff_t = {(a, b): flip(diff_t[a, b], a=a, b=b) for a in range(2) for b in range(2)}
    lots, came = gate(lots, came)
    lots_c = [flip(m, e=1) for m in lots]

    rows = sd // NZ
    own = dot(jnp.concatenate([normed, normed_c], 0), jnp.concatenate([stay[0], came[0]], 0), ((0,), (0,)))
    far = dot(jnp.concatenate([*lots, *lots_c], 0), jnp.concatenate([stay[1], came[1]], 0), ((0,), (0,)))
    own, far, diff_t = gate(own, far, diff_t)
    term = ((own + far) * (1.0 / math.sqrt(toks * NZ * 4))).astype(BF).reshape(NZ, rows, blk)

    terms = lax.all_to_all(term, "dp", 0, 0, axis_index_groups=RINGS, tiled=True)
    grad = jnp.sum(terms.astype(F32), axis=0)
    grad_proj = jnp.zeros((rows // 4, wide), F32)
    for a in range(2):
        for e in range(2):
            p = piece(grad, 2 * (l ^ a) + (h ^ e), rows // 4, 0)
            p = move(p, lambda z, l, c, x, h: (z, l ^ a, h ^ e, x, c))
            grad_proj = put(grad_proj, p, 2 * (l ^ a) + (c ^ e), 1)

    diff, order = [], []
    for b in range(2):
        for a in range(2):
            diff.append(diff_t[a, b])
            order.append(2 * (l ^ a) + (h ^ b))
    share = sd // (NX * 2)
    to = [(x + k) % NX for k in range(NX)] + [h] * 4
    parts = backs(jnp.stack(to + order).astype(jnp.int32), diff, z_own, projector, share)
    back = parts[0].astype(F32)
    for i in (5, 4, 3, 7, 2, 6, 1):
        back = back + shift(parts[i], k=i // 2, b=i % 2).astype(F32)
    stat = (back[share] + back[share + 1])[:, None]
    xhat = piece(student, mp, share, 1).astype(F32) * inv
    dxhat = back[:share].T * piece(gain_f, mp, share, 0)
    return grad_proj, (inv * (dxhat - xhat * stat)).astype(BF)


def solution(mesh):
    in_specs = (P("dp", "mp"), P("mp", "dp"), P("dp", "mp"), P("dp", None), P(), P(None, "mp"))
    out_specs = (P("dp", "mp"), P("dp", "mp"))
    return jax.shard_map(
        on_device, mesh=mesh, in_specs=in_specs, out_specs=out_specs, check_vma=False
    )
```

```python
import functools
import math

import jax
import jax.numpy as jnp
from jax import lax
from jax.experimental import pallas as pl
from jax.experimental.pallas import tpu as pltpu
from jax.sharding import PartitionSpec as P

NZ, NX = 8, 4
VMEM = 56 * 2**20
BF, F32 = jnp.bfloat16, jnp.float32


def flat(z, l, c, x, h):
    return ((z * 2 + l) * 2 + c) * (NX * 2) + x * 2 + h


PLACES = [
    (z, l, c, x, h)
    for z in range(NZ)
    for l in range(2)
    for c in range(2)
    for x in range(NX)
    for h in range(2)
]


RINGS = [[z * 4 + i for z in range(NZ)] for i in range(4)]
LINES = [[x * 2 + h for x in range(NX)] for h in range(2)]
SQUARES = [
    [flat(z, l, c, x, h) for l in range(2) for h in range(2)]
    for z in range(NZ)
    for c in range(2)
    for x in range(NX)
]


def move(value, to):
    return lax.ppermute(value, ("dp", "mp"), [(flat(*p), flat(*to(*p))) for p in PLACES])


def flip(value, a=0, b=0, e=0):
    if not a + b + e:
        return value
    return move(value, lambda z, l, c, x, h: (z, l ^ a, c ^ e, x, h ^ b))


def shift(value, s=0, k=0, b=0):
    return move(value, lambda z, l, c, x, h: ((z + s) % NZ, l, c, (x + k) % NX, h ^ b))


def after(value, *first):
    return lax.optimization_barrier((value, *first))[0]


def gate(*values):
    return lax.optimization_barrier(values)


def dot(a, b, dims):
    return lax.dot_general(a, b, (dims, ((), ())), preferred_element_type=F32)


def piece(value, index, size, axis):
    return lax.dynamic_slice_in_dim(value, index * size, size, axis)


def put(whole, value, index, axis):
    return lax.dynamic_update_slice_in_dim(whole, value, index * value.shape[axis], axis)


def difference_kernel(at, m0, m1, m2, m3, d0, stay, leave, *pieces):
    l, h, c = at[0], at[1], at[2]
    for b in range(2):
        for a in range(2):
            own = 2 * b + a
            total = m0[own].astype(F32) + m1[own].astype(F32) + m2[own].astype(F32) + m3[own].astype(F32)
            diff = (d0[2 * (l ^ a) + (h ^ b)].astype(F32) - total).astype(BF)
            pieces[2 * b + a][...] = diff

            @pl.when((h ^ b) == c)
            def _():
                stay[a] = diff

            @pl.when((h ^ b) != c)
            def _():
                leave[a] = diff


def difference(at, sums, d0):
    one = jax.ShapeDtypeStruct(d0.shape[1:], BF)
    two = jax.ShapeDtypeStruct((2, *d0.shape[1:]), BF)
    return pl.pallas_call(
        difference_kernel,
        out_shape=[two, two, one, one, one, one],
        grid=(1,),
        in_specs=[pl.BlockSpec(memory_space=pltpu.SMEM)] + [whole(d0.shape)] * 5,
        out_specs=[whole(two.shape)] * 2 + [whole(one.shape)] * 4,
        compiler_params=pltpu.CompilerParams(vmem_limit_bytes=VMEM),
    )(at, *sums, d0)


def whole(shape):
    return pl.BlockSpec(shape, lambda *i: (0,) * len(shape))


def products_kernel(n, kept, at, *refs):
    attn, a_h, a_l, a_lh = refs[kept:kept + 4]
    blocks = refs[kept + 4:kept + 4 + 2 * n]
    outs, (made, sems) = refs[kept + 4 + 2 * n:-2], refs[-2:]
    toks = attn.shape[0]

    def run(turn):
        for i in range(n):
            w_h, w_o = blocks[2 * i + turn], blocks[2 * i + 1 - turn]
            for a, (near, far) in enumerate(((attn, a_h), (a_l, a_lh))):
                part = jnp.dot(near[...], w_h[...], preferred_element_type=F32)
                part = part + jnp.dot(far[...], w_o[...], preferred_element_type=F32)
                made[i, a * toks:(a + 1) * toks] = part.astype(BF)

    pl.when(at[0] == 0)(lambda: run(0))
    pl.when(at[0] != 0)(lambda: run(1))
    for i in range(n):
        for k in range(NX):

            @pl.when(at[1 + 2 * i] == k)
            def _():
                copy = pltpu.make_async_copy(made.at[i], outs[k].at[at[2 + 2 * i]], sems.at[i])
                copy.start()
                copy.wait()


def products(at, kept, heads, blocks):
    n = len(blocks) // 2
    toks, blk = heads[0].shape[0], blocks[0].shape[1]
    anywhere = pl.BlockSpec(memory_space=pl.ANY)
    return pl.pallas_call(
        functools.partial(products_kernel, n, len(kept)),
        out_shape=[jax.ShapeDtypeStruct((2, 2 * toks, blk), BF)] * NX,
        grid=(1,),
        in_specs=[pl.BlockSpec(memory_space=pltpu.SMEM)]
        + [anywhere] * len(kept)
        + [whole(m.shape) for m in (*heads, *blocks)],
        out_specs=[anywhere] * NX,
        scratch_shapes=[pltpu.VMEM((n, 2 * toks, blk), BF), pltpu.SemaphoreType.DMA((n,))],
        input_output_aliases={1 + k: k for k in range(len(kept))},
        compiler_params=pltpu.CompilerParams(vmem_limit_bytes=VMEM),
        cost_estimate=pl.CostEstimate(
            flops=n * 8 * toks * blk * heads[0].shape[1], bytes_accessed=8 * 2**20, transcendentals=0
        ),
    )(at, *kept, *heads, *blocks)


def back_kernel(sd, at, d0, d1, d2, d3, z_own, rows_p, *refs):
    outs, (tail, turned) = refs[:-2], refs[-2:]
    share = rows_p.shape[0] // 2
    step = pl.program_id(0)
    toks, blk = d0.shape
    columns = [pl.ds(pl.multiple_of(at[8 + q] * blk, blk), blk) for q in range(4)]
    pieces = (d0, d1, d2, d3)

    @pl.when(step == 0)
    def _():
        stat = 0.0
        for d, q in zip(pieces, columns):
            turned[q] = d[...].astype(F32).T.astype(BF)
            stat = stat + jnp.sum(d[...].astype(F32) * z_own[:, q], axis=-1, keepdims=True)
        stat = jnp.broadcast_to(stat / sd, (toks, 128)).T[:16]
        high = stat.astype(BF)
        low = (stat - high.astype(F32)).astype(BF)
        row = lax.broadcasted_iota(jnp.int32, stat.shape, 0)
        kept = jnp.where(row == 0, high.astype(F32), jnp.where(row == 1, low.astype(F32), 0.0))
        tail[...] = kept.astype(BF)

    part = jnp.dot(rows_p[...], turned[...], preferred_element_type=F32)
    near, far = part[:share], part[share:]
    halves = jnp.where(at[4] == 0, near, far), jnp.where(at[4] == 0, far, near)
    for k, out in enumerate(outs):

        @pl.when(step == k // 2)
        def _():
            out[:share] = halves[k % 2].astype(BF)
            out[share:] = tail[...]


def backs(at, diffs, z_own, projector, share):
    toks, blk = diffs[0].shape
    sd, wide = projector.shape
    one = jax.ShapeDtypeStruct((share + 16, toks), BF)
    return pl.pallas_call(
        functools.partial(back_kernel, sd),
        out_shape=[one] * 8,
        grid_spec=pltpu.PrefetchScalarGridSpec(
            num_scalar_prefetch=1,
            grid=(NX,),
            in_specs=[whole(d.shape) for d in diffs]
            + [whole(z_own.shape), pl.BlockSpec((2 * share, wide), lambda i, at: (at[i], 0))],
            out_specs=[whole(one.shape)] * 8,
            scratch_shapes=[pltpu.VMEM((16, toks), BF), pltpu.VMEM((wide, toks), BF)],
        ),
        compiler_params=pltpu.CompilerParams(vmem_limit_bytes=VMEM),
        cost_estimate=pl.CostEstimate(
            flops=2 * toks * sd * wide, bytes_accessed=10 * 2**20, transcendentals=0
        ),
    )(at, *diffs, z_own, projector)


def on_device(attn, out_proj, resid, student, gain, projector):
    toks, wide = resid.shape
    sd = student.shape[1]
    blk = out_proj.shape[1]
    dp, mp = lax.axis_index("dp"), lax.axis_index("mp")
    z, l, c = dp // 4, (dp // 2) % 2, dp % 2
    x, h = mp // 2, mp % 2

    w0 = move(
        out_proj,
        lambda z, l, c, x, h: (z, l, c, x, h) if c == h else (z, l, h, x, 1 - h),
    )

    v = student.astype(F32)
    inv = lax.rsqrt(jnp.mean(v * v, axis=-1, keepdims=True) + 1e-05)
    gain_f = gain.astype(F32)
    normed = (v * inv * gain_f).astype(BF)

    ring, pair, outs = {}, {}, []

    def swap(*slots):
        for s in slots:
            pair[s] = flip(ring[s], e=1)

    def multiply(*slots):
        place = [c ^ h]
        for s in slots:
            to = (z + s) % NZ
            place += [(to // 2 - x) % NX, (to % 2) ^ h]
        blocks = [w for s in slots for w in (ring[s], pair[s])]
        return products(jnp.stack(place).astype(jnp.int32), outs, [attn, a_h, a_l, a_lh], blocks)

    ring[0], attn = gate(w0, attn)
    ring[1], ring[-1] = shift(ring[0], s=-1), shift(ring[0], s=1)
    a_l, a_lh = flip(attn, a=1), flip(attn, a=1, b=1)

    ring, normed = gate(ring, normed)
    ring[2], ring[-2] = shift(ring[1], s=-1), shift(ring[-1], s=1)
    swap(0)
    z_own = dot(normed, projector, ((1,), (0,)))
    d0 = (z_own - resid.astype(F32)).astype(BF)
    d0 = jnp.stack([d0[:, q * blk:(q + 1) * blk] for q in range(4)])


    ring, pair, attn, a_l, a_lh, normed, d0, z_own = gate(ring, pair, attn, a_l, a_lh, normed, d0, z_own)
    ring[3], ring[-3] = shift(ring[2], s=-1), shift(ring[-2], s=1)
    a_h = flip(attn, b=1)
    swap(1, -1)

    lots = normed[:toks // 2], normed[toks // 2:]

    ring, pair, normed, d0, a_h, lots = gate(ring, pair, normed, d0, a_h, lots)
    ring[4] = shift(ring[3], s=-1)
    swap(2, -2, 3, -3)
    outs = multiply(0, 1, -1)
    outs = multiply(2, -2, 3, -3)

    ring, outs, normed = gate(ring, outs, normed)
    swap(4)
    normed_c = flip(normed, e=1)
    outs = multiply(4)

    outs, lots, d0, normed_c = gate(outs, lots, d0, normed_c)
    sums = [shift(outs[k], k=k) if k else outs[k] for k in range(NX)]
    lots = flip(lots[0], a=1), flip(lots[1], a=1, b=1)
    d0_t = lax.all_to_all(d0, ("dp", "mp"), 0, 0, axis_index_groups=SQUARES, tiled=True)
    sums, lots, d0_t = gate(sums, lots, d0_t)
    stay, leave, *diff_t = difference(
        jnp.stack([l, h, c]).astype(jnp.int32),
        [m.reshape(4, toks, blk) for m in sums],
        d0_t,
    )
    diff_t = {(a, b): diff_t[2 * b + a] for a in range(2) for b in range(2)}

    came = flip(leave, e=1)
    diff_t = {(a, b): flip(diff_t[a, b], a=a, b=b) for a in range(2) for b in range(2)}
    lots, came = gate(lots, came)
    lots_c = [flip(m, e=1) for m in lots]

    rows = sd // NZ
    own = dot(jnp.concatenate([normed, normed_c], 0), jnp.concatenate([stay[0], came[0]], 0), ((0,), (0,)))
    far = dot(jnp.concatenate([*lots, *lots_c], 0), jnp.concatenate([stay[1], came[1]], 0), ((0,), (0,)))
    own, far, diff_t = gate(own, far, diff_t)
    term = ((own + far) * (1.0 / math.sqrt(toks * NZ * 4))).astype(BF).reshape(NZ, rows, blk)

    terms = lax.all_to_all(term, "dp", 0, 0, axis_index_groups=RINGS, tiled=True)
    grad = jnp.sum(terms.astype(F32), axis=0)
    grad_proj = jnp.zeros((rows // 4, wide), F32)
    for a in range(2):
        for e in range(2):
            p = piece(grad, 2 * (l ^ a) + (h ^ e), rows // 4, 0)
            p = move(p, lambda z, l, c, x, h: (z, l ^ a, h ^ e, x, c))
            grad_proj = put(grad_proj, p, 2 * (l ^ a) + (c ^ e), 1)

    diff, order = [], []
    for b in range(2):
        for a in range(2):
            diff.append(diff_t[a, b])
            order.append(2 * (l ^ a) + (h ^ b))
    share = sd // (NX * 2)
    to = [(x + k) % NX for k in range(NX)] + [h] * 4
    parts = backs(jnp.stack(to + order).astype(jnp.int32), diff, z_own, projector, share)
    back = parts[0].astype(F32)
    for i in (5, 4, 3, 7, 2, 6, 1):
        back = back + shift(parts[i], k=i // 2, b=i % 2).astype(F32)
    stat = (back[share] + back[share + 1])[:, None]
    xhat = piece(student, mp, share, 1).astype(F32) * inv
    dxhat = back[:share].T * piece(gain_f, mp, share, 0)
    return grad_proj, (inv * (dxhat - xhat * stat)).astype(BF)


def solution(mesh):
    in_specs = (P("dp", "mp"), P("mp", "dp"), P("dp", "mp"), P("dp", None), P(), P(None, "mp"))
    out_specs = (P("dp", "mp"), P("dp", "mp"))
    return jax.shard_map(
        on_device, mesh=mesh, in_specs=in_specs, out_specs=out_specs, check_vma=False
    )
```
